32 devices in a mesh: blk: 8 (over y, x, core), narrow: 4 (over z).
Axes of the slice: x: 2, y: 2, z: 4, core: 2. Of those that a mesh axis runs over, the one named last changes fastest.
Arguments:
- student_bytes: bfloat16 [16384, 2048], P(('blk', 'narrow')), may hold values from -6 to 6
- student_weight: bfloat16 [2048, 1024], replicated, may hold values from -0.125 to 0.125
- teacher_rows: bfloat16 [4096, 8192], P('blk', 'narrow'), may hold values from -6 to 6
- teacher_weight: bfloat16 [8192, 1024], P('narrow'), may hold values from -0.0625 to 0.0625
- span_lengths: int32 [8, 512], P('blk'), may hold values from 1 to 16, 2048 in all within a row
- span_scale: float32 [4096], P(('blk', 'narrow')), may hold values from 20 to 4000
- positives: int32 [4096], P(('blk', 'narrow')), may hold values from 0 to 2047
Outputs:
- loss_mean: float32 [], replicated
- grad_bytes: bfloat16 [16384, 2048], P(('blk', 'narrow'))
- grad_teacher_weight: float32 [8192, 1024], P('narrow')
The draws below stay inside these ranges and needn't reach their ends.
All inputs are finite; a program needn't handle non-finite values.
Results may differ from the reference program's by a relative error of at most 0.007.
The reference program's roundings to bfloat16 on the way (of `projected`, `student`, `teacher`, `score_grads`, `span_grad`, `byte_grad` and `teacher_grad`) count: a program that leaves them out, or rounds other values in their place, can miss the bound.
Values may be sent and summed in bfloat16 or wider, within the bound.
No kernel may reach another device: no remote copies, remote signals or barrier semaphores. Data moves between devices by JAX's collectives and lax.ppermute only.
A program may use at most 128 MiB of HBM per device.

```python
import math
import jax
import jax.numpy as jnp
import numpy as np
from jax import lax

E = 1024
DS = 2048
DT = 8192
S_DEV = 128
SPAN_BYTES = 4
MOST_BYTES = 16
STOPS = 4
BYTE_DEV = 512
S_BLK = 512
SPANS = 4096
BYTES = 16384
N_BLK = 8
N_NARROW = 4


def draw_span_scale(key, part):
    key = jax.random.fold_in(key, 11)
    highest = 160.0
    lowest = 20.0
    uniform_draw = jax.random.uniform(key, (SPANS,), jnp.float32)
    position = jnp.arange(SPANS, dtype=jnp.float32) / SPANS
    fraction = 0.85 * position + 0.15 * uniform_draw
    return jnp.exp(jnp.log(lowest) + fraction * (jnp.log(highest) - jnp.log(lowest)))


def plant(values, own_key, low, high):
    shape = values.shape
    index_at = [jax.random.randint(jax.random.fold_in(own_key, axis), (), 0, shape[axis]) for axis in range(len(shape))]
    values = values.at[tuple(index_at)].set(low)
    longest = shape.index(max(shape))
    index_at[longest] = (index_at[longest] + 1) % shape[longest]
    return values.at[tuple(index_at)].set(high)


def levels(rng, dims, pieces, smallest, high):
    gain = 1.0
    for axis_at, parts in pieces:
        steps = jax.random.uniform(jax.random.fold_in(jax.random.fold_in(rng, 6), axis_at), (parts,), jnp.float32, smallest / len(pieces), high / len(pieces))
        gain = gain * jnp.repeat(jnp.exp(steps), dims[axis_at] // parts).reshape((-1,) + (1,) * (len(dims) - 1 - axis_at))
    return gain


def profile(number_of, total, limit, lean):
    weights = [(1 << 20) // math.isqrt(standing ** lean) + 1 for standing in range(2, number_of + 1)]
    rest, holding = total - limit - (number_of - 1), [1] * (number_of - 1)
    while rest > 0:
        candidates = [i for i in range(number_of - 1) if holding[i] < limit]
        mass, budget = sum([weights[i] for i in candidates]), rest
        for i in candidates:
            addition = min(limit - holding[i], max(1, budget * weights[i] // mass), rest)
            holding[i] = holding[i] + addition
            rest = rest - addition
    return np.array([limit] + holding)


def ragged(rng, amount, total, most, skew):
    if amount == 2:
        one = jax.random.randint(rng, (), max(1, total - most), min(most, total - 1) + 1)
        return jnp.stack([one, total - one])
    sizes = jnp.asarray(profile(amount, total, most, skew), jnp.int32)
    twos = (amount - 1) // 2
    donor, receiver = sizes[1:1 + 2 * twos:2], sizes[2:2 + 2 * twos:2]
    margin = jnp.minimum(donor - 1, most - receiver)
    moved = jax.random.randint(jax.random.fold_in(rng, 1), (twos,), 0, 1 << 20) % (margin + 1)
    sizes = sizes.at[1:1 + 2 * twos:2].set(donor - moved).at[2:2 + 2 * twos:2].set(receiver + moved)
    return sizes[jax.random.permutation(jax.random.fold_in(rng, 2), amount)]


def bell_draw(rng, dims, width, reach, shards=(), held_as=jnp.bfloat16):
    result = jax.random.normal(rng, dims, jnp.float32) * width
    if len(shards) > 0:
        result = levels(rng, dims, shards, -0.22, 0.18) * result
    return jnp.clip(result, min=-reach, max=reach).astype(held_as)


def setup_inputs(seed: int = 0) -> dict:
    key_of = jax.random.split(jax.random.key(seed), 8)
    return {
        "student_bytes": bell_draw(key_of[0], (BYTES, DS), 1.0, 6.0, ((0, 32),)),
        "student_weight": bell_draw(key_of[1], (DS, E), DS ** -0.5, 0.125),
        "teacher_rows": bell_draw(key_of[2], (SPANS, DT), 1.0, 6.0, ((0, 8), (1, 4))),
        "teacher_weight": bell_draw(key_of[3], (DT, E), DT ** -0.5, 0.0625, ((0, 4),)),
        "span_lengths": jax.vmap(lambda own: ragged(own, S_BLK, SPAN_BYTES * S_BLK, MOST_BYTES, 2))(jax.random.split(key_of[4], N_BLK)).reshape((N_BLK, S_BLK)).astype(jnp.int32),
        "span_scale": draw_span_scale(jax.random.fold_in(key_of[7], 71), 0),
        "positives": plant(jax.random.randint(key_of[6], (SPANS,), 0, STOPS * S_BLK), jax.random.fold_in(key_of[6], 1), 0, (STOPS * S_BLK) - 1).astype(jnp.int32),
    }


EPS = 1e-06

def normalize(values):
    inv_rms = lax.rsqrt(lax.optimization_barrier(jnp.mean(values * values, axis=-1, keepdims=True)) + EPS)
    return (values * inv_rms, inv_rms)

def norm_back(upstream, normed, inv_rms):
    inner_mean = lax.optimization_barrier(jnp.mean(upstream * normed, axis=-1, keepdims=True))
    return inv_rms * (upstream - normed * inner_mean)

def owner_order(values):
    return values.reshape(N_BLK, S_DEV, N_NARROW).transpose(0, 2, 1).reshape(N_BLK, S_BLK)

def reference(student_bytes, student_weight, teacher_rows, teacher_weight, span_lengths, span_scale, positives):
    group_bytes = BYTE_DEV * N_NARROW
    projected = jnp.dot(student_bytes, student_weight, preferred_element_type=jnp.float32).astype(jnp.bfloat16)
    projected = projected.reshape(N_BLK, group_bytes, E)
    byte_ends = jnp.cumsum(span_lengths, axis=1).astype(jnp.int32)
    byte_starts = (byte_ends - span_lengths).astype(jnp.int32)
    span_ends = owner_order(byte_ends)
    starts = owner_order(byte_starts)
    ordered_lengths = owner_order(span_lengths)
    byte_pos = jnp.arange(group_bytes, dtype=jnp.int32)

    def make_table(start_row, end_row):
        inside = (byte_pos[None, :] >= start_row[:, None]) & (byte_pos[None, :] < end_row[:, None])
        return inside.astype(jnp.bfloat16)

    def pool_group(inputs):
        row_block, start_row, end_row = inputs
        return jnp.dot(make_table(start_row, end_row), row_block, preferred_element_type=jnp.float32)
    pooled = lax.map(pool_group, (projected, starts, span_ends))
    lengths_float = ordered_lengths.astype(jnp.float32)[:, :, None]
    span_mean = pooled / lengths_float
    student_full, student_rms = normalize(span_mean)
    student = student_full.astype(jnp.bfloat16)
    teacher_proj = jnp.dot(teacher_rows, teacher_weight, preferred_element_type=jnp.float32).reshape(N_BLK, S_BLK, E)
    teacher_full, teacher_rms = normalize(teacher_proj)
    teacher = teacher_full.astype(jnp.bfloat16)
    scale_rows = span_scale.reshape(N_BLK, S_BLK)
    positive_rows = positives.reshape(N_BLK, S_BLK)
    column = jnp.arange(STOPS * S_BLK, dtype=jnp.int32)

    def group_step(state, group):
        dteacher_sum, loss_sum = state
        owners = ((group - jnp.arange(STOPS, dtype=jnp.int32)) % N_BLK).astype(jnp.int32)
        window_keys = teacher[owners].reshape(STOPS * S_BLK, E)
        queries = student[group]
        factor = scale_rows[group][:, None] / E
        scores = jnp.dot(queries, window_keys.T, preferred_element_type=jnp.float32) * factor
        row_max = lax.optimization_barrier(jnp.max(scores, axis=1, keepdims=True))
        log_total = row_max[:, 0] + jnp.log(lax.optimization_barrier(jnp.sum(jnp.exp(scores - row_max), axis=1)))
        positive_mask = column[None, :] == positive_rows[group][:, None]
        picked = lax.optimization_barrier(jnp.sum(jnp.where(positive_mask, scores, 0.0), axis=1))
        loss_sum = loss_sum + jnp.sum(log_total - picked)
        score_grads = ((jnp.exp(scores - log_total[:, None]) - positive_mask.astype(jnp.float32)) * factor).astype(jnp.bfloat16)
        dstudent = jnp.dot(score_grads, window_keys, preferred_element_type=jnp.float32)
        key_grads = jnp.dot(score_grads.T, queries, preferred_element_type=jnp.float32).reshape(STOPS, S_BLK, E)
        dteacher_sum = dteacher_sum.at[owners].add(key_grads)
        return ((dteacher_sum, loss_sum), dstudent)
    initial = (jnp.zeros((N_BLK, S_BLK, E), jnp.float32), jnp.zeros((), jnp.float32))
    (dteacher, loss_sum), dstudent = lax.scan(group_step, initial, jnp.arange(N_BLK, dtype=jnp.int32))
    span_grad = (norm_back(dstudent, student_full, student_rms) / lengths_float).astype(jnp.bfloat16)

    def spread_group(inputs):
        grad_block, start_row, end_row = inputs
        return jnp.dot(make_table(start_row, end_row).T, grad_block, preferred_element_type=jnp.float32).astype(jnp.bfloat16)
    byte_grad = lax.map(spread_group, (span_grad, starts, span_ends)).reshape(BYTES, E)
    grad_bytes = jnp.dot(byte_grad, student_weight.T, preferred_element_type=jnp.float32).astype(jnp.bfloat16)
    teacher_grad = norm_back(dteacher, teacher_full, teacher_rms).astype(jnp.bfloat16).reshape(SPANS, E)
    grad_teacher_weight = jnp.dot(teacher_rows.T, teacher_grad, preferred_element_type=jnp.float32)
    loss_mean = loss_sum / SPANS
    return (loss_mean, grad_bytes, grad_teacher_weight)
```

```python
import jax
import jax.numpy as jnp
from jax import lax
from jax.sharding import PartitionSpec as P

STOPS = 4
EPS = 1e-06
BF16 = jnp.bfloat16
F32 = jnp.float32


def normalize(values):
    inv_rms = lax.rsqrt(jnp.mean(values * values, axis=-1, keepdims=True) + EPS)
    return (values * inv_rms, inv_rms)


def norm_back(upstream, normed, inv_rms):
    inner_mean = jnp.mean(upstream * normed, axis=-1, keepdims=True)
    return inv_rms * (upstream - normed * inner_mean)


def contract_first(left, right):
    return lax.dot_general(left, right, (((0,), (0,)), ((), ())), preferred_element_type=F32)


def contract_last(left, right):
    return lax.dot_general(left, right, (((1,), (1,)), ((), ())), preferred_element_type=F32)


def permute_blk(x, target):
    count = lax.axis_size("blk")
    return lax.ppermute(x, "blk", [(i, target(i) % count) for i in range(count)])


def sibling(x):
    return permute_blk(x, lambda i: i ^ 1)


def gather_narrow(x):
    count = lax.axis_size("narrow")
    index = lax.axis_index("narrow")
    out = jnp.zeros((count,) + x.shape, x.dtype)
    out = lax.dynamic_update_index_in_dim(out, x, index, 0)
    for by in range(1, count):
        came = lax.ppermute(x, "narrow", [(i, (i + by) % count) for i in range(count)])
        out = lax.dynamic_update_index_in_dim(out, came, lax.rem(index + count - by, count), 0)
    return out


def shards(
    student_bytes, student_weight, teacher_rows, teacher_weight, span_lengths, span_scale, positives
):
    span_dev = span_scale.shape[0]
    embed_width = student_weight.shape[1]
    lanes = lax.axis_size("narrow")
    blocks = lax.axis_size("blk")
    chips = blocks // 2
    lane = lax.axis_index("narrow")
    block = lax.axis_index("blk")
    core = lax.rem(block, 2)
    chip = lax.div(block, 2)
    span_block = span_dev * lanes
    byte_dev = student_bytes.shape[0]
    feats = teacher_rows.shape[1]
    half = feats // 2

    own_half = lax.dynamic_slice_in_dim(teacher_rows, core * half, half, 1)
    sibling_half = sibling(lax.dynamic_slice_in_dim(teacher_rows, (1 - core) * half, half, 1))

    factor_own = span_scale / embed_width
    small = jnp.stack([factor_own, positives.astype(F32)])
    small = gather_narrow(small)
    factor = small[:, 0].reshape(span_block)
    positive = small[:, 1].reshape(span_block)

    byte_lengths = span_lengths[0]
    byte_ends = jnp.cumsum(byte_lengths)
    byte_starts = byte_ends - byte_lengths

    def owner_order(values):
        return values.reshape(span_dev, lanes).T.reshape(span_block)

    lengths = owner_order(byte_lengths)
    ends = owner_order(byte_ends)
    starts = owner_order(byte_starts)
    lengths_f = lengths.astype(F32)[:, None]
    first = lane * byte_dev
    last = first + byte_dev
    byte_pos = first + jnp.arange(byte_dev, dtype=jnp.int32)
    span_table = (
        (byte_pos[None, :] >= starts[:, None]) & (byte_pos[None, :] < ends[:, None])
    ).astype(BF16)
    cut_left = (starts < first) & (ends > first)
    cut_right = (starts < last) & (ends > last)
    left_end = jnp.sum(jnp.where(cut_left, ends, 0))
    right_start = jnp.sum(jnp.where(cut_right, starts - last, 0)) + last
    edge_table = jnp.stack([byte_pos < left_end, byte_pos >= right_start]).astype(BF16)
    projected = jnp.dot(student_bytes, student_weight, preferred_element_type=F32).astype(BF16)
    edges = jnp.dot(edge_table, projected, preferred_element_type=F32)
    from_right = lax.ppermute(edges[0:1], "narrow", [(i + 1, i) for i in range(lanes - 1)])
    from_left = lax.ppermute(edges[1:2], "narrow", [(i, i + 1) for i in range(lanes - 1)])
    partial = jnp.dot(span_table, projected, preferred_element_type=F32)
    pooled = (
        partial
        + jnp.where(cut_right[:, None], from_right, 0.0)
        + jnp.where(cut_left[:, None], from_left, 0.0)
    )
    student_full, student_rms = normalize(pooled / lengths_f)
    begins_here = (starts >= first) & (starts < last)
    student_sparse = jnp.where(begins_here[:, None], student_full, 0.0).astype(BF16)
    student_shard = lax.psum_scatter(student_sparse, "narrow", scatter_dimension=0, tiled=True)
    student = lax.all_gather(student_shard, "narrow", axis=0, tiled=True)

    teacher_rows_late, _ = lax.optimization_barrier((teacher_rows, projected))
    teacher_proj = lax.psum_scatter(
        jnp.dot(teacher_rows_late, teacher_weight, preferred_element_type=F32),
        "narrow",
        scatter_dimension=0,
        tiled=True,
    )
    teacher_full, teacher_rms = normalize(teacher_proj)
    teacher = teacher_full.astype(BF16)

    def following(x):
        ahead = permute_blk(x, lambda i: i - 2)
        mixed = permute_blk(x, lambda i: i - 1 if i % 2 else i - 3)
        return ahead, mixed

    ahead, mixed = following(student)
    other = sibling(ahead)
    student_window = [student, ahead, mixed, other]
    mixed_stop = jnp.where(core == 1, 3, 1)
    window_stops = [0, 2, mixed_stop, 4 - mixed_stop]

    def following_small(x):
        ahead, mixed = following(x)
        other = permute_blk(x, lambda i: i - 3 if i % 2 else i - 1)
        return [x, ahead, mixed, other]

    window_factor = following_small(factor)
    window_positive = following_small(positive)

    keys = [teacher] + [permute_blk(teacher, lambda i, k=k: i + k) for k in range(1, STOPS)]
    near = jnp.arange(span_dev, dtype=F32)[None, :] + (lane * span_dev).astype(F32)
    parts = []
    maxes = []
    for stop in range(STOPS):
        scores = contract_last(student, keys[stop]) * factor[:, None]
        hit = near + stop * span_block == positive[:, None]
        picked = jnp.sum(jnp.where(hit, scores, 0.0), axis=1)
        parts.append((scores, picked))
        maxes.append(jnp.max(scores, axis=1))
    row_max = maxes[0]
    for stop in range(1, STOPS):
        row_max = jnp.maximum(row_max, maxes[stop])
    row_sum = sum(jnp.sum(jnp.exp(s - row_max[:, None]), axis=1) for s, _ in parts)
    picked = sum(p for _, p in parts)
    stats = gather_narrow(jnp.stack([row_max, row_sum, picked]))
    top = jnp.max(stats[:, 0], axis=0)
    log_total = top + jnp.log(jnp.sum(stats[:, 1] * jnp.exp(stats[:, 0] - top), axis=0))
    loss = jnp.sum(log_total - jnp.sum(stats[:, 2], axis=0)).reshape(1)
    window_log_total = following_small(log_total)

    dteacher = jnp.zeros((span_dev, embed_width), F32)
    column = jnp.arange(span_dev, dtype=jnp.int32)[:, None] + lane * span_dev
    for at in range(4):
        scale = window_factor[at][None, :]
        scores = contract_last(teacher, student_window[at]) * scale
        column_here = (column + window_stops[at] * span_block).astype(F32)
        hit = (column_here == window_positive[at][None, :]).astype(F32)
        grads = ((jnp.exp(scores - window_log_total[at][None, :]) - hit) * scale).astype(BF16)
        dteacher = dteacher + jnp.dot(grads, student_window[at], preferred_element_type=F32)
    teacher_grad = norm_back(dteacher, teacher_full, teacher_rms).astype(BF16)
    teacher_grads = lax.all_gather(teacher_grad, "narrow", axis=0, tiled=True)
    sibling_grads = sibling(teacher_grads)

    weight_part = contract_first(own_half, teacher_grads) + contract_first(
        sibling_half, sibling_grads
    )
    slice_rows = half // chips
    narrowed = weight_part.astype(BF16)
    total = lax.dynamic_slice_in_dim(weight_part, chip * slice_rows, slice_rows, 0)
    came = []
    for by in range(1, chips):
        target = lax.rem(chip + by, chips)
        piece = lax.dynamic_slice_in_dim(narrowed, target * slice_rows, slice_rows, 0)
        came.append(permute_blk(piece, lambda i, by=by: i + 2 * by))
    for piece in came:
        total = total + piece.astype(F32)
    total = total.astype(BF16)
    grad_weight = jnp.zeros((feats, embed_width), F32)
    for by in range(chips):
        piece = total if by == 0 else permute_blk(total, lambda i, by=by: i + 2 * by)
        twin = sibling(piece)
        at = lax.rem(chip + chips - by, chips) * slice_rows
        grad_weight = lax.dynamic_update_slice_in_dim(
            grad_weight, piece.astype(F32), core * half + at, 0
        )
        grad_weight = lax.dynamic_update_slice_in_dim(
            grad_weight, twin.astype(F32), (1 - core) * half + at, 0
        )

    teacher_block = lax.all_gather(teacher, "narrow", axis=0, tiled=True)
    back = permute_blk(teacher_block, lambda i: i + 2)
    back_mixed = permute_blk(teacher_block, lambda i: i + 3 if i % 2 else i + 1)
    back_other = sibling(back)
    teacher_window = [teacher_block, back, back_mixed, back_other]
    back_stop = jnp.where(core == 1, 1, 3)
    back_stops = [0, 2, back_stop, 4 - back_stop]
    columns = jnp.arange(span_block, dtype=jnp.int32)[None, :]
    dstudent = jnp.zeros((span_block, embed_width), F32)
    for at in range(4):
        scores = contract_last(student, teacher_window[at]) * factor[:, None]
        column_here = (columns + back_stops[at] * span_block).astype(F32)
        hit = (column_here == positive[:, None]).astype(F32)
        grads = ((jnp.exp(scores - log_total[:, None]) - hit) * factor[:, None]).astype(BF16)
        dstudent = dstudent + jnp.dot(grads, teacher_window[at], preferred_element_type=F32)
    span_grad = (norm_back(dstudent, student_full, student_rms) / lengths_f).astype(BF16)
    byte_grad = contract_first(span_table, span_grad).astype(BF16)
    grad_bytes = contract_last(byte_grad, student_weight).astype(BF16)

    step = 1
    while step < blocks:
        loss = loss + permute_blk(loss, lambda i, step=step: i ^ step)
        step *= 2
    loss_mean = loss[0] / (span_block * blocks)
    return (loss_mean, grad_bytes, grad_weight)


def solution(mesh):
    return jax.shard_map(
        shards,
        mesh=mesh,
        in_specs=(
            P(("blk", "narrow"), None),
            P(),
            P("blk", "narrow"),
            P("narrow", None),
            P("blk", None),
            P(("blk", "narrow")),
            P(("blk", "narrow")),
        ),
        out_specs=(P(), P(("blk", "narrow"), None), P("narrow", None)),
        check_vma=False,
    )
```

```python
import functools

import jax
import jax.numpy as jnp
from jax import lax
from jax.experimental import pallas as pl
from jax.experimental.pallas import tpu as pltpu
from jax.sharding import PartitionSpec as P

STOPS = 4
EPS = 1e-06
BF16 = jnp.bfloat16
F32 = jnp.float32


def normalize(values):
    inv_rms = lax.rsqrt(jnp.mean(values * values, axis=-1, keepdims=True) + EPS)
    return (values * inv_rms, inv_rms)


def norm_back(upstream, normed, inv_rms):
    inner_mean = jnp.mean(upstream * normed, axis=-1, keepdims=True)
    return inv_rms * (upstream - normed * inner_mean)


def contract_first(left, right):
    return lax.dot_general(left, right, (((0,), (0,)), ((), ())), preferred_element_type=F32)


def contract_last(left, right):
    return lax.dot_general(left, right, (((1,), (1,)), ((), ())), preferred_element_type=F32)


def permute_blk(x, target):
    count = lax.axis_size("blk")
    return lax.ppermute(x, "blk", [(i, target(i) % count) for i in range(count)])


def sibling(x):
    return permute_blk(x, lambda i: i ^ 1)


def gather_narrow(x):
    count = lax.axis_size("narrow")
    index = lax.axis_index("narrow")
    out = jnp.zeros((count,) + x.shape, x.dtype)
    out = lax.dynamic_update_index_in_dim(out, x, index, 0)
    for by in range(1, count):
        came = lax.ppermute(x, "narrow", [(i, (i + by) % count) for i in range(count)])
        out = lax.dynamic_update_index_in_dim(out, came, lax.rem(index + count - by, count), 0)
    return out


def following(x):
    ahead = permute_blk(x, lambda i: i - 2)
    mixed = permute_blk(x, lambda i: i - 1 if i % 2 else i - 3)
    return ahead, mixed


def following_other(x):
    return permute_blk(x, lambda i: i - 3 if i % 2 else i - 1)


def scatter_narrow(x, rows):
    count = lax.axis_size("narrow")
    index = lax.axis_index("narrow")
    total = lax.dynamic_slice_in_dim(x, index * rows, rows, 0)
    for by in range(1, count):
        target = lax.rem(index + by, count)
        piece = lax.dynamic_slice_in_dim(x, target * rows, rows, 0)
        total += lax.ppermute(piece, "narrow", [(i, (i + by) % count) for i in range(count)])
    return total


def teacher_side(rows, teacher_ref, rms_ref, s0_ref, s1_ref, s2_ref, s3_ref, small_ref, out_ref):
    teacher = teacher_ref[...]
    dteacher = None
    for at, ref in enumerate((s0_ref, s1_ref, s2_ref, s3_ref)):
        scale = small_ref[at : at + 1, :]
        log_total = small_ref[4 + at : 5 + at, :]
        column = small_ref[8 + at : 9 + at, :].astype(jnp.int32)
        scores = contract_last(teacher, ref[...]) * scale
        here = lax.broadcasted_iota(jnp.int32, scores.shape, 0) + pl.program_id(0) * rows
        hit = jnp.where(here == column, 1.0, 0.0)
        grads = ((jnp.exp(scores - log_total) - hit) * scale).astype(BF16)
        term = jnp.dot(grads, ref[...], preferred_element_type=F32)
        dteacher = term if dteacher is None else dteacher + term
    full = teacher.astype(F32)
    inner_mean = jnp.mean(dteacher * full, axis=-1, keepdims=True)
    out_ref[...] = (rms_ref[...] * (dteacher - full * inner_mean)).astype(BF16)


def teacher_grads_of(teacher, rms, window, small):
    span_block, width = teacher.shape
    rows = 256
    whole = pl.BlockSpec((span_block, width), lambda i: (0, 0))
    part = pl.BlockSpec((rows, width), lambda i: (i, 0))
    return pl.pallas_call(
        functools.partial(teacher_side, rows),
        grid=(span_block // rows,),
        in_specs=[part, pl.BlockSpec((rows, 1), lambda i: (i, 0))] + [whole] * 4 + [pl.BlockSpec(small.shape, lambda i: (0, 0))],
        out_specs=part,
        out_shape=jax.ShapeDtypeStruct((span_block, width), BF16),
        compiler_params=pltpu.CompilerParams(vmem_limit_bytes=48 * 1024 * 1024),
        cost_estimate=pl.CostEstimate(
            flops=16 * span_block * span_block * width,
            bytes_accessed=14 * span_block * width,
            transcendentals=4 * span_block * span_block,
        ),
        name="teacher_side",
    )(teacher, rms, *window, small)


def student_side(student_ref, full_ref, scalar_ref, own_ref, others_ref, out_ref):
    student = student_ref[...]
    scale = scalar_ref[:, 0:1]
    log_total = scalar_ref[:, 1:2]

    def term(keys, at):
        column = scalar_ref[:, 4 + at : 5 + at].astype(jnp.int32)
        scores = contract_last(student, keys) * scale
        here = lax.broadcasted_iota(jnp.int32, scores.shape, 1)
        hit = jnp.where(here == column, 1.0, 0.0)
        grads = ((jnp.exp(scores - log_total) - hit) * scale).astype(BF16)
        return jnp.dot(grads, keys, preferred_element_type=F32)

    dstudent = term(own_ref[...], 0)
    for at in range(others_ref.shape[0]):
        dstudent = dstudent + term(others_ref[at], 1 + at)
    full = full_ref[...]
    inner_mean = jnp.mean(dstudent * full, axis=-1, keepdims=True)
    grad = scalar_ref[:, 2:3] * (dstudent - full * inner_mean) / scalar_ref[:, 3:4]
    out_ref[...] = grad.astype(BF16)


def span_grads_of(student, full, scalars, own, others):
    span_block, width = student.shape
    rows = 256
    part = pl.BlockSpec((rows, width), lambda i: (i, 0))
    return pl.pallas_call(
        student_side,
        grid=(span_block // rows,),
        in_specs=[
            part,
            part,
            pl.BlockSpec((rows, scalars.shape[1]), lambda i: (i, 0)),
            pl.BlockSpec(own.shape, lambda i: (0, 0)),
            pl.BlockSpec(others.shape, lambda i: (0, 0, 0)),
        ],
        out_specs=part,
        out_shape=jax.ShapeDtypeStruct((span_block, width), BF16),
        compiler_params=pltpu.CompilerParams(vmem_limit_bytes=48 * 1024 * 1024),
        cost_estimate=pl.CostEstimate(
            flops=16 * span_block * span_block * width,
            bytes_accessed=16 * span_block * width,
            transcendentals=4 * span_block * span_block,
        ),
        name="student_side",
    )(student, full, scalars, own, others)


def shards(
    student_bytes, student_weight, teacher_rows, teacher_weight, span_lengths, span_scale, positives
):
    span_dev = span_scale.shape[0]
    embed_width = student_weight.shape[1]
    lanes = lax.axis_size("narrow")
    blocks = lax.axis_size("blk")
    chips = blocks // 2
    lane = lax.axis_index("narrow")
    block = lax.axis_index("blk")
    core = lax.rem(block, 2)
    chip = lax.div(block, 2)
    span_block = span_dev * lanes
    byte_dev = student_bytes.shape[0]
    feats = teacher_rows.shape[1]
    half = feats // 2

    own_half = lax.dynamic_slice_in_dim(teacher_rows, core * half, half, 1)
    sibling_half = sibling(lax.dynamic_slice_in_dim(teacher_rows, (1 - core) * half, half, 1))

    teacher_part = jnp.dot(teacher_rows, teacher_weight, preferred_element_type=F32)
    student_bytes, teacher_part = lax.optimization_barrier((student_bytes, teacher_part))
    teacher_proj = lax.psum_scatter(teacher_part, "narrow", scatter_dimension=0, tiled=True)

    small = gather_narrow(jnp.stack([span_scale / embed_width, positives.astype(F32)]))
    small = small.transpose(1, 0, 2).reshape(2, span_block)
    ahead_small, mixed_small = following(small)
    other_small = following_other(small)

    byte_lengths = span_lengths[0]
    byte_ends = jnp.cumsum(byte_lengths)
    byte_starts = byte_ends - byte_lengths

    def owner_order(values):
        return values.reshape(span_dev, lanes).T.reshape(span_block)

    lengths = owner_order(byte_lengths)
    ends = owner_order(byte_ends)
    starts = owner_order(byte_starts)
    lengths_f = lengths.astype(F32)[:, None]
    first = lane * byte_dev
    last = first + byte_dev
    byte_pos = first + jnp.arange(byte_dev, dtype=jnp.int32)
    span_table = (
        (byte_pos[None, :] >= starts[:, None]) & (byte_pos[None, :] < ends[:, None])
    ).astype(BF16)
    cut_left = (starts < first) & (ends > first)
    cut_right = (starts < last) & (ends > last)
    left_end = jnp.sum(jnp.where(cut_left, ends, 0))
    right_start = jnp.sum(jnp.where(cut_right, starts - last, 0)) + last
    edge_table = jnp.stack([byte_pos < left_end, byte_pos >= right_start]).astype(BF16)
    projected = jnp.dot(student_bytes, student_weight, preferred_element_type=F32).astype(BF16)
    edges = jnp.dot(edge_table, projected, preferred_element_type=F32)
    from_right = lax.ppermute(edges[0:1], "narrow", [(i + 1, i) for i in range(lanes - 1)])
    from_left = lax.ppermute(edges[1:2], "narrow", [(i, i + 1) for i in range(lanes - 1)])
    partial = jnp.dot(span_table, projected, preferred_element_type=F32)
    pooled = (
        partial
        + jnp.where(cut_right[:, None], from_right, 0.0)
        + jnp.where(cut_left[:, None], from_left, 0.0)
    )
    student_full, student_rms = normalize(pooled / lengths_f)
    begins_here = (starts >= first) & (starts < last)
    student_sparse = jnp.where(begins_here[:, None], student_full, 0.0).astype(BF16)
    student_shard = scatter_narrow(student_sparse, span_dev)
    student_shard, teacher_proj, small, ahead_small, mixed_small, other_small = (
        lax.optimization_barrier(
            (student_shard, teacher_proj, small, ahead_small, mixed_small, other_small)
        )
    )
    factor, positive = small[0], small[1]
    window_small = [small, ahead_small, mixed_small, other_small]
    student = lax.all_gather(student_shard, "narrow", axis=0, tiled=True)

    teacher_full, teacher_rms = normalize(teacher_proj)
    teacher = teacher_full.astype(BF16)
    keys = jnp.concatenate(
        [teacher] + [permute_blk(teacher, lambda i, k=k: i + k) for k in range(1, STOPS)], axis=0
    )
    teacher, student, keys = lax.optimization_barrier((teacher, student, keys))
    teacher_block = lax.all_gather(teacher, "narrow", axis=0, tiled=True)

    ahead, mixed = following(student)
    other = sibling(ahead)
    student_window = [student, ahead, mixed, other]
    mixed_stop = jnp.where(core == 1, 3, 1)
    window_stops = [jnp.int32(0), jnp.int32(2), mixed_stop, 4 - mixed_stop]

    near = jnp.arange(STOPS * span_dev, dtype=jnp.int32)
    near = (near // span_dev) * span_block + lane * span_dev + near % span_dev
    hit = near.astype(F32)[None, :] == positive[:, None]
    scores = contract_last(student, keys) * factor[:, None]
    picked = jnp.sum(jnp.where(hit, scores, 0.0), axis=1)
    row_max = jnp.max(scores, axis=1)
    row_sum = jnp.sum(jnp.exp(scores - row_max[:, None]), axis=1)
    rms_row = jnp.pad(teacher_rms[:, 0], (0, span_block - span_dev))
    stats = gather_narrow(jnp.stack([row_max, row_sum, picked, rms_row]))
    block_rms = stats[:, 3, :span_dev].reshape(span_block, 1)
    top = jnp.max(stats[:, 0], axis=0)
    log_total = top + jnp.log(jnp.sum(stats[:, 1] * jnp.exp(stats[:, 0] - top), axis=0))
    loss = jnp.sum(log_total - jnp.sum(stats[:, 2], axis=0))
    note = jnp.concatenate([log_total, jnp.broadcast_to(loss, (128,))])
    notes = [note, *following(note), following_other(note)]
    window_log_total = [x[:span_block] for x in notes]

    ahead_loss, mixed_loss, other_loss = [x[span_block] for x in notes[1:]]
    four = jnp.stack(
        [
            loss,
            jnp.where(core == 1, other_loss, mixed_loss),
            ahead_loss,
            jnp.where(core == 1, mixed_loss, other_loss),
        ]
    )
    turned = [four] + [permute_blk(four, lambda i, by=by: i - by) for by in range(4, blocks, 4)]
    turned = jnp.concatenate(turned * 2)
    in_order = lax.dynamic_slice_in_dim(turned, lax.rem(blocks - block, blocks), blocks)
    loss_mean = jnp.sum(in_order) / (span_block * blocks)

    others, teacher_block = lax.optimization_barrier((keys[span_dev:], teacher_block))
    others = lax.all_gather(others, "narrow", axis=0)

    small = jnp.stack(
        [x[0] for x in window_small]
        + window_log_total
        + [x[1] - (stop * span_block).astype(F32) for x, stop in zip(window_small, window_stops)]
    )
    teacher_grads = teacher_grads_of(teacher_block, block_rms, student_window, small)
    sibling_grads = sibling(teacher_grads)

    weight_part = contract_first(own_half, teacher_grads) + contract_first(
        sibling_half, sibling_grads
    )
    slice_rows = half // chips
    narrowed = weight_part.astype(BF16)
    total = lax.dynamic_slice_in_dim(weight_part, chip * slice_rows, slice_rows, 0)
    came = []
    for by in range(1, chips):
        target = lax.rem(chip + by, chips)
        piece = lax.dynamic_slice_in_dim(narrowed, target * slice_rows, slice_rows, 0)
        came.append(permute_blk(piece, lambda i, by=by: i + 2 * by))
    for piece in came:
        total = total + piece.astype(F32)
    total = (total + 0.0 * loss_mean).astype(BF16)
    place = positive.astype(jnp.int32)
    stop, place = place // span_block, place % span_block
    at_lane, at_row = place // span_dev, place % span_dev
    columns = [jnp.where(stop == 0, place, -1)] + [
        jnp.where((stop > 0) & (at_lane == i), (stop - 1) * span_dev + at_row, -1)
        for i in range(lanes)
    ]
    scalars = jnp.stack(
        [factor, log_total + 0.0 * weight_part[0, 0], student_rms[:, 0], lengths_f[:, 0]]
        + [x.astype(F32) for x in columns],
        axis=1,
    )
    span_grad = span_grads_of(student, student_full, scalars, teacher_block, others)
    byte_grad = contract_first(span_table, span_grad).astype(BF16)
    grad_bytes = contract_last(byte_grad, student_weight).astype(BF16)

    zero = 0.0 * grad_bytes[0, 0].astype(F32)
    grad_weight = jnp.tile(total.astype(F32), (2 * chips, 1))
    for by in range(chips):
        piece = total if by == 0 else permute_blk(total, lambda i, by=by: i + 2 * by)
        twin = sibling(piece)
        at = lax.rem(chip + chips - by, chips) * slice_rows
        grad_weight = lax.dynamic_update_slice_in_dim(
            grad_weight, piece.astype(F32), core * half + at, 0
        )
        grad_weight = lax.dynamic_update_slice_in_dim(
            grad_weight, twin.astype(F32) + (zero if by == chips - 1 else 0.0), (1 - core) * half + at, 0
        )

    return (loss_mean, grad_bytes, grad_weight)


def solution(mesh):
    return jax.shard_map(
        shards,
        mesh=mesh,
        in_specs=(
            P(("blk", "narrow"), None),
            P(),
            P("blk", "narrow"),
            P("narrow", None),
            P("blk", None),
            P(("blk", "narrow")),
            P(("blk", "narrow")),
        ),
        out_specs=(P(), P(("blk", "narrow"), None), P("narrow", None)),
        check_vma=False,
    )
```

```python
import functools

import jax
import jax.numpy as jnp
from jax import lax
from jax.experimental import pallas as pl
from jax.experimental.pallas import tpu as pltpu
from jax.sharding import PartitionSpec as P

STOPS = 4
MOST_BYTES = 16
EPS = 1e-06
BF16 = jnp.bfloat16
F32 = jnp.float32


def normalize(values):
    inv_rms = lax.rsqrt(jnp.mean(values * values, axis=-1, keepdims=True) + EPS)
    return (values * inv_rms, inv_rms)


def norm_back(upstream, normed, inv_rms):
    inner_mean = jnp.mean(upstream * normed, axis=-1, keepdims=True)
    return inv_rms * (upstream - normed * inner_mean)


def contract_first(left, right):
    return lax.dot_general(left, right, (((0,), (0,)), ((), ())), preferred_element_type=F32)


def contract_last(left, right):
    return lax.dot_general(left, right, (((1,), (1,)), ((), ())), preferred_element_type=F32)


def permute_blk(x, target):
    count = lax.axis_size("blk")
    return lax.ppermute(x, "blk", [(i, target(i) % count) for i in range(count)])


def sibling(x):
    return permute_blk(x, lambda i: i ^ 1)


def gather_narrow(x):
    count = lax.axis_size("narrow")
    index = lax.axis_index("narrow")
    out = jnp.zeros((count,) + x.shape, x.dtype)
    out = lax.dynamic_update_index_in_dim(out, x, index, 0)
    for by in range(1, count):
        came = lax.ppermute(x, "narrow", [(i, (i + by) % count) for i in range(count)])
        out = lax.dynamic_update_index_in_dim(out, came, lax.rem(index + count - by, count), 0)
    return out


def following(x):
    ahead = permute_blk(x, lambda i: i - 2)
    mixed = permute_blk(x, lambda i: i - 1 if i % 2 else i - 3)
    return ahead, mixed


def following_other(x):
    return permute_blk(x, lambda i: i - 3 if i % 2 else i - 1)


def scatter_narrow(x, rows):
    count = lax.axis_size("narrow")
    index = lax.axis_index("narrow")
    total = lax.dynamic_slice_in_dim(x, index * rows, rows, 0)
    for by in range(1, count):
        target = lax.rem(index + by, count)
        piece = lax.dynamic_slice_in_dim(x, target * rows, rows, 0)
        total += lax.ppermute(piece, "narrow", [(i, (i + by) % count) for i in range(count)])
    return total


def teacher_side(rows, teacher_ref, rms_ref, s0_ref, s1_ref, s2_ref, s3_ref, small_ref, out_ref):
    teacher = teacher_ref[...]
    dteacher = None
    for at, ref in enumerate((s0_ref, s1_ref, s2_ref, s3_ref)):
        scale = small_ref[at : at + 1, :]
        log_total = small_ref[4 + at : 5 + at, :]
        column = small_ref[8 + at : 9 + at, :].astype(jnp.int32)
        scores = contract_last(teacher, ref[...]) * scale
        here = lax.broadcasted_iota(jnp.int32, scores.shape, 0) + pl.program_id(0) * rows
        hit = jnp.where(here == column, 1.0, 0.0)
        grads = ((jnp.exp(scores - log_total) - hit) * scale).astype(BF16)
        term = jnp.dot(grads, ref[...], preferred_element_type=F32)
        dteacher = term if dteacher is None else dteacher + term
    full = teacher.astype(F32)
    inner_mean = jnp.mean(dteacher * full, axis=-1, keepdims=True)
    out_ref[...] = (rms_ref[...] * (dteacher - full * inner_mean)).astype(BF16)


def teacher_grads_of(teacher, rms, window, small):
    span_block, width = teacher.shape
    rows = 256
    whole = pl.BlockSpec((span_block, width), lambda i: (0, 0))
    part = pl.BlockSpec((rows, width), lambda i: (i, 0))
    return pl.pallas_call(
        functools.partial(teacher_side, rows),
        grid=(span_block // rows,),
        in_specs=[part, pl.BlockSpec((rows, 1), lambda i: (i, 0))] + [whole] * 4 + [pl.BlockSpec(small.shape, lambda i: (0, 0))],
        out_specs=part,
        out_shape=jax.ShapeDtypeStruct((span_block, width), BF16),
        compiler_params=pltpu.CompilerParams(vmem_limit_bytes=48 * 1024 * 1024),
        cost_estimate=pl.CostEstimate(
            flops=16 * span_block * span_block * width,
            bytes_accessed=14 * span_block * width,
            transcendentals=4 * span_block * span_block,
        ),
        name="teacher_side",
    )(teacher, rms, *window, small)


def student_side(student_ref, full_ref, scalar_ref, own_ref, others_ref, out_ref):
    student = student_ref[...]
    scale = scalar_ref[:, 0:1]
    log_total = scalar_ref[:, 1:2]

    def term(keys, at):
        column = scalar_ref[:, 4 + at : 5 + at].astype(jnp.int32)
        scores = contract_last(student, keys) * scale
        here = lax.broadcasted_iota(jnp.int32, scores.shape, 1)
        hit = jnp.where(here == column, 1.0, 0.0)
        grads = ((jnp.exp(scores - log_total) - hit) * scale).astype(BF16)
        return jnp.dot(grads, keys, preferred_element_type=F32)

    dstudent = term(own_ref[...], 0)
    for at in range(others_ref.shape[0]):
        dstudent = dstudent + term(others_ref[at], 1 + at)
    full = full_ref[...]
    inner_mean = jnp.mean(dstudent * full, axis=-1, keepdims=True)
    grad = scalar_ref[:, 2:3] * (dstudent - full * inner_mean) / scalar_ref[:, 3:4]
    out_ref[...] = grad.astype(BF16)


def span_grads_of(student, full, scalars, own, others):
    span_block, width = student.shape
    rows = 256
    part = pl.BlockSpec((rows, width), lambda i: (i, 0))
    return pl.pallas_call(
        student_side,
        grid=(span_block // rows,),
        in_specs=[
            part,
            part,
            pl.BlockSpec((rows, scalars.shape[1]), lambda i: (i, 0)),
            pl.BlockSpec(own.shape, lambda i: (0, 0)),
            pl.BlockSpec(others.shape, lambda i: (0, 0, 0)),
        ],
        out_specs=part,
        out_shape=jax.ShapeDtypeStruct((span_block, width), BF16),
        compiler_params=pltpu.CompilerParams(vmem_limit_bytes=48 * 1024 * 1024),
        cost_estimate=pl.CostEstimate(
            flops=16 * span_block * span_block * width,
            bytes_accessed=16 * span_block * width,
            transcendentals=4 * span_block * span_block,
        ),
        name="student_side",
    )(student, full, scalars, own, others)


def assemble(order_ref, *refs):
    for at, ref in enumerate(refs[:-1]):

        @pl.when(pl.program_id(0) == at)
        def _(ref=ref):
            refs[-1][...] = ref[...].astype(F32)


def assembled(order, pieces):
    rows, width = pieces[0].shape
    count = len(pieces)
    return pl.pallas_call(
        assemble,
        grid_spec=pltpu.PrefetchScalarGridSpec(
            num_scalar_prefetch=1,
            grid=(count,),
            in_specs=[pl.BlockSpec((rows, width), lambda i, order: (0, 0))] * count,
            out_specs=pl.BlockSpec((rows, width), lambda i, order: (order[i], 0)),
        ),
        out_shape=jax.ShapeDtypeStruct((count * rows, width), F32),
        compiler_params=pltpu.CompilerParams(vmem_limit_bytes=32 * 1024 * 1024),
        cost_estimate=pl.CostEstimate(
            flops=count * rows * width, bytes_accessed=6 * count * rows * width, transcendentals=0
        ),
        name="assemble",
    )(order, *pieces)


def shards(
    student_bytes, student_weight, teacher_rows, teacher_weight, span_lengths, span_scale, positives
):
    span_dev = span_scale.shape[0]
    embed_width = student_weight.shape[1]
    lanes = lax.axis_size("narrow")
    blocks = lax.axis_size("blk")
    chips = blocks // 2
    lane = lax.axis_index("narrow")
    block = lax.axis_index("blk")
    core = lax.rem(block, 2)
    chip = lax.div(block, 2)
    span_block = span_dev * lanes
    byte_dev = student_bytes.shape[0]
    feats = teacher_rows.shape[1]
    half = feats // 2

    own_half = lax.dynamic_slice_in_dim(teacher_rows, core * half, half, 1)
    sibling_half = sibling(lax.dynamic_slice_in_dim(teacher_rows, (1 - core) * half, half, 1))

    spread = jnp.arange(MOST_BYTES, dtype=jnp.int32)
    edge_bytes = jnp.concatenate(
        [
            lax.ppermute(student_bytes[-MOST_BYTES:], "narrow", [(i, i + 1) for i in range(lanes - 1)]),
            lax.ppermute(student_bytes[:MOST_BYTES], "narrow", [(i + 1, i) for i in range(lanes - 1)]),
        ],
        axis=0,
    )

    teacher_part = jnp.dot(teacher_rows, teacher_weight, preferred_element_type=F32)
    student_bytes, teacher_part = lax.optimization_barrier((student_bytes, teacher_part))
    teacher_proj = lax.psum_scatter(teacher_part, "narrow", scatter_dimension=0, tiled=True)

    small = gather_narrow(jnp.stack([span_scale / embed_width, positives.astype(F32)]))
    small = small.transpose(1, 0, 2).reshape(2, span_block)
    ahead_small, mixed_small = following(small)
    other_small = following_other(small)

    byte_lengths = span_lengths[0]
    byte_ends = jnp.cumsum(byte_lengths)
    byte_starts = byte_ends - byte_lengths

    def owner_order(values):
        return values.reshape(span_dev, lanes).T.reshape(span_block)

    lengths = owner_order(byte_lengths)
    ends = owner_order(byte_ends)
    starts = owner_order(byte_starts)
    lengths_f = lengths.astype(F32)[:, None]
    first = lane * byte_dev
    last = first + byte_dev
    byte_pos = first + jnp.arange(byte_dev, dtype=jnp.int32)
    span_table = (
        (byte_pos[None, :] >= starts[:, None]) & (byte_pos[None, :] < ends[:, None])
    ).astype(BF16)
    edge_pos = jnp.concatenate([first - MOST_BYTES + spread, last + spread])
    edge_table = (
        (edge_pos[None, :] >= starts[:, None]) & (edge_pos[None, :] < ends[:, None])
    ).astype(BF16)
    projected = jnp.dot(student_bytes, student_weight, preferred_element_type=F32).astype(BF16)
    projected_edge = jnp.dot(edge_bytes, student_weight, preferred_element_type=F32).astype(BF16)
    pooled = jnp.dot(span_table, projected, preferred_element_type=F32) + jnp.dot(
        edge_table, projected_edge, preferred_element_type=F32
    )
    student_full, student_rms = normalize(pooled / lengths_f)
    begins_here = (starts >= first) & (starts < last)
    student_sparse = jnp.where(begins_here[:, None], student_full, 0.0).astype(BF16)
    student_sparse, small, ahead_small, mixed_small, other_small, own_half = (
        lax.optimization_barrier(
            (student_sparse, small, ahead_small, mixed_small, other_small, own_half)
        )
    )
    student_shard = scatter_narrow(student_sparse, span_dev)
    factor, positive = small[0], small[1]
    window_small = [small, ahead_small, mixed_small, other_small]
    student_shard, teacher_proj = lax.optimization_barrier((student_shard, teacher_proj))
    student = lax.all_gather(student_shard, "narrow", axis=0, tiled=True)

    teacher_full, teacher_rms = normalize(teacher_proj)
    teacher = teacher_full.astype(BF16)
    others = jnp.concatenate(
        [permute_blk(teacher, lambda i, k=k: i + k) for k in range(1, STOPS)], axis=0
    )
    keys = jnp.concatenate([teacher, others], axis=0)
    teacher, student, keys, others = lax.optimization_barrier((teacher, student, keys, others))
    teacher_block = lax.all_gather(teacher, "narrow", axis=0, tiled=True)

    ahead, mixed = following(student)
    mixed_stop = jnp.where(core == 1, 3, 1)
    window_stops = [jnp.int32(0), jnp.int32(2), mixed_stop, 4 - mixed_stop]

    near = jnp.arange(STOPS * span_dev, dtype=jnp.int32)
    near = (near // span_dev) * span_block + lane * span_dev + near % span_dev
    hit = near.astype(F32)[None, :] == positive[:, None]
    scores = contract_last(student, keys) * factor[:, None]
    picked = jnp.sum(jnp.where(hit, scores, 0.0), axis=1)
    row_max = jnp.max(scores, axis=1)
    row_sum = jnp.sum(jnp.exp(scores - row_max[:, None]), axis=1)
    rms_row = jnp.pad(teacher_rms[:, 0], (0, span_block - span_dev))
    stats = gather_narrow(jnp.stack([row_max, row_sum, picked, rms_row]))
    block_rms = stats[:, 3, :span_dev].reshape(span_block, 1)
    top = jnp.max(stats[:, 0], axis=0)
    log_total = top + jnp.log(jnp.sum(stats[:, 1] * jnp.exp(stats[:, 0] - top), axis=0))
    loss = jnp.sum(log_total - jnp.sum(stats[:, 2], axis=0))
    ahead, log_total = lax.optimization_barrier((ahead, log_total))
    student_window = [student, ahead, mixed, sibling(ahead)]
    note = jnp.concatenate([log_total, jnp.broadcast_to(loss, (128,))])
    notes = [note, *following(note), following_other(note)]
    window_log_total = [x[:span_block] for x in notes]

    spots = jnp.arange(128, dtype=jnp.int32)
    terms = jnp.zeros((128,), F32)
    for x, stop in zip(notes, window_stops):
        terms = jnp.where(spots == lax.rem(block + stop, blocks), x[span_block:], terms)
    own_terms = terms
    for by in range(4, blocks, 4):
        terms = terms + permute_blk(own_terms, lambda i, by=by: i - by)
    loss_mean = jnp.sum(terms) / (span_block * blocks)

    others, log_total = lax.optimization_barrier((others, log_total))
    others = lax.all_gather(others, "narrow", axis=0)

    small = jnp.stack(
        [x[0] for x in window_small]
        + window_log_total
        + [x[1] - (stop * span_block).astype(F32) for x, stop in zip(window_small, window_stops)]
    )
    teacher_grads = teacher_grads_of(teacher_block, block_rms, student_window, small)
    sibling_grads = sibling(teacher_grads)

    weight_part = contract_first(own_half, teacher_grads) + contract_first(
        sibling_half, sibling_grads
    )
    slice_rows = half // chips
    narrowed = weight_part.astype(BF16)
    total = lax.dynamic_slice_in_dim(weight_part, chip * slice_rows, slice_rows, 0)
    came = []
    for by in range(1, chips):
        target = lax.rem(chip + by, chips)
        piece = lax.dynamic_slice_in_dim(narrowed, target * slice_rows, slice_rows, 0)
        came.append(permute_blk(piece, lambda i, by=by: i + 2 * by))
    for piece in came:
        total = total + piece.astype(F32)
    total = (total + 0.0 * loss_mean).astype(BF16)
    place = positive.astype(jnp.int32)
    stop, place = place // span_block, place % span_block
    at_lane, at_row = place // span_dev, place % span_dev
    columns = [jnp.where(stop == 0, place, -1)] + [
        jnp.where((stop > 0) & (at_lane == i), (stop - 1) * span_dev + at_row, -1)
        for i in range(lanes)
    ]
    scalars = jnp.stack(
        [factor, log_total + 0.0 * weight_part[0, 0], student_rms[:, 0], lengths_f[:, 0]]
        + [x.astype(F32) for x in columns],
        axis=1,
    )
    span_grad = span_grads_of(student, student_full, scalars, teacher_block, others)
    byte_grad = contract_first(span_table, span_grad).astype(BF16)
    grad_bytes = contract_last(byte_grad, student_weight).astype(BF16)

    pieces = []
    order = []
    for by in range(chips):
        piece = total if by == 0 else permute_blk(total, lambda i, by=by: i + 2 * by)
        if by > 0:
            made = span_grad if by == chips - 1 else grad_bytes
            piece, _ = lax.optimization_barrier((piece, made))
        pieces += [piece, sibling(piece)]
        at = lax.rem(chip + chips - by, chips)
        order += [core * chips + at, (1 - core) * chips + at]
    grad_weight = assembled(jnp.stack(order), pieces)
    return (loss_mean, grad_bytes, grad_weight)


def solution(mesh):
    return jax.shard_map(
        shards,
        mesh=mesh,
        in_specs=(
            P(("blk", "narrow"), None),
            P(),
            P("blk", "narrow"),
            P("narrow", None),
            P("blk", None),
            P(("blk", "narrow")),
            P(("blk", "narrow")),
        ),
        out_specs=(P(), P(("blk", "narrow"), None), P("narrow", None)),
        check_vma=False,
    )
```

```python
import functools

import jax
import jax.numpy as jnp
from jax import lax
from jax.experimental import pallas as pl
from jax.experimental.pallas import tpu as pltpu
from jax.sharding import PartitionSpec as P

STOPS = 4
MOST_BYTES = 16
EPS = 1e-06
BF16 = jnp.bfloat16
F32 = jnp.float32


def normalize(values):
    inv_rms = lax.rsqrt(jnp.mean(values * values, axis=-1, keepdims=True) + EPS)
    return (values * inv_rms, inv_rms)


def norm_back(upstream, normed, inv_rms):
    inner_mean = jnp.mean(upstream * normed, axis=-1, keepdims=True)
    return inv_rms * (upstream - normed * inner_mean)


def contract_first(left, right):
    return lax.dot_general(left, right, (((0,), (0,)), ((), ())), preferred_element_type=F32)


def contract_last(left, right):
    return lax.dot_general(left, right, (((1,), (1,)), ((), ())), preferred_element_type=F32)


def permute_blk(x, target):
    count = lax.axis_size("blk")
    return lax.ppermute(x, "blk", [(i, target(i) % count) for i in range(count)])


def sibling(x):
    return permute_blk(x, lambda i: i ^ 1)


def gather_narrow(x):
    count = lax.axis_size("narrow")
    index = lax.axis_index("narrow")
    out = jnp.zeros((count,) + x.shape, x.dtype)
    out = lax.dynamic_update_index_in_dim(out, x, index, 0)
    for by in range(1, count):
        came = lax.ppermute(x, "narrow", [(i, (i + by) % count) for i in range(count)])
        out = lax.dynamic_update_index_in_dim(out, came, lax.rem(index + count - by, count), 0)
    return out


def following(x):
    ahead = permute_blk(x, lambda i: i - 2)
    mixed = permute_blk(x, lambda i: i - 1 if i % 2 else i - 3)
    return ahead, mixed


def following_other(x):
    return permute_blk(x, lambda i: i - 3 if i % 2 else i - 1)


def scatter_narrow(x, rows):
    count = lax.axis_size("narrow")
    index = lax.axis_index("narrow")
    total = lax.dynamic_slice_in_dim(x, index * rows, rows, 0)
    for by in range(1, count):
        target = lax.rem(index + by, count)
        piece = lax.dynamic_slice_in_dim(x, target * rows, rows, 0)
        total += lax.ppermute(piece, "narrow", [(i, (i + by) % count) for i in range(count)])
    return total


def teacher_side(rows, teacher_ref, rms_ref, s0_ref, s1_ref, s2_ref, s3_ref, small_ref, out_ref):
    teacher = teacher_ref[...]
    dteacher = None
    for at, ref in enumerate((s0_ref, s1_ref, s2_ref, s3_ref)):
        scale = small_ref[at : at + 1, :]
        log_total = small_ref[4 + at : 5 + at, :]
        column = small_ref[8 + at : 9 + at, :].astype(jnp.int32)
        scores = contract_last(teacher, ref[...]) * scale
        here = lax.broadcasted_iota(jnp.int32, scores.shape, 0) + pl.program_id(0) * rows
        hit = jnp.where(here == column, 1.0, 0.0)
        grads = ((jnp.exp(scores - log_total) - hit) * scale).astype(BF16)
        term = jnp.dot(grads, ref[...], preferred_element_type=F32)
        dteacher = term if dteacher is None else dteacher + term
    full = teacher.astype(F32)
    inner_mean = jnp.mean(dteacher * full, axis=-1, keepdims=True)
    out_ref[...] = (rms_ref[...] * (dteacher - full * inner_mean)).astype(BF16)


def teacher_grads_of(teacher, rms, window, small):
    span_block, width = teacher.shape
    rows = 256
    whole = pl.BlockSpec((span_block, width), lambda i: (0, 0))
    part = pl.BlockSpec((rows, width), lambda i: (i, 0))
    return pl.pallas_call(
        functools.partial(teacher_side, rows),
        grid=(span_block // rows,),
        in_specs=[part, pl.BlockSpec((rows, 1), lambda i: (i, 0))] + [whole] * 4 + [pl.BlockSpec(small.shape, lambda i: (0, 0))],
        out_specs=part,
        out_shape=jax.ShapeDtypeStruct((span_block, width), BF16),
        compiler_params=pltpu.CompilerParams(vmem_limit_bytes=48 * 1024 * 1024),
        cost_estimate=pl.CostEstimate(
            flops=16 * span_block * span_block * width,
            bytes_accessed=14 * span_block * width,
            transcendentals=4 * span_block * span_block,
        ),
        name="teacher_side",
    )(teacher, rms, *window, small)


def student_side(student_ref, full_ref, scalar_ref, own_ref, others_ref, out_ref):
    student = student_ref[...]
    scale = scalar_ref[:, 0:1]
    log_total = scalar_ref[:, 1:2]

    def term(keys, at):
        column = scalar_ref[:, 4 + at : 5 + at].astype(jnp.int32)
        scores = contract_last(student, keys) * scale
        here = lax.broadcasted_iota(jnp.int32, scores.shape, 1)
        hit = jnp.where(here == column, 1.0, 0.0)
        grads = ((jnp.exp(scores - log_total) - hit) * scale).astype(BF16)
        return jnp.dot(grads, keys, preferred_element_type=F32)

    dstudent = term(own_ref[...], 0)
    for at in range(others_ref.shape[0]):
        dstudent = dstudent + term(others_ref[at], 1 + at)
    full = full_ref[...]
    inner_mean = jnp.mean(dstudent * full, axis=-1, keepdims=True)
    grad = scalar_ref[:, 2:3] * (dstudent - full * inner_mean) / scalar_ref[:, 3:4]
    out_ref[...] = grad.astype(BF16)


def span_grads_of(student, full, scalars, own, others):
    span_block, width = student.shape
    rows = 256
    part = pl.BlockSpec((rows, width), lambda i: (i, 0))
    return pl.pallas_call(
        student_side,
        grid=(span_block // rows,),
        in_specs=[
            part,
            part,
            pl.BlockSpec((rows, scalars.shape[1]), lambda i: (i, 0)),
            pl.BlockSpec(own.shape, lambda i: (0, 0)),
            pl.BlockSpec(others.shape, lambda i: (0, 0, 0)),
        ],
        out_specs=part,
        out_shape=jax.ShapeDtypeStruct((span_block, width), BF16),
        compiler_params=pltpu.CompilerParams(vmem_limit_bytes=48 * 1024 * 1024),
        cost_estimate=pl.CostEstimate(
            flops=16 * span_block * span_block * width,
            bytes_accessed=16 * span_block * width,
            transcendentals=4 * span_block * span_block,
        ),
        name="student_side",
    )(student, full, scalars, own, others)


def assemble(order_ref, *refs):
    for at, ref in enumerate(refs[:-1]):

        @pl.when(pl.program_id(0) == at)
        def _(ref=ref):
            refs[-1][...] = ref[...].astype(F32)


def assembled(order, pieces):
    rows, width = pieces[0].shape
    count = len(pieces)
    return pl.pallas_call(
        assemble,
        grid_spec=pltpu.PrefetchScalarGridSpec(
            num_scalar_prefetch=1,
            grid=(count,),
            in_specs=[pl.BlockSpec((rows, width), lambda i, order: (0, 0))] * count,
            out_specs=pl.BlockSpec((rows, width), lambda i, order: (order[i], 0)),
        ),
        out_shape=jax.ShapeDtypeStruct((count * rows, width), F32),
        compiler_params=pltpu.CompilerParams(vmem_limit_bytes=32 * 1024 * 1024),
        cost_estimate=pl.CostEstimate(
            flops=count * rows * width, bytes_accessed=6 * count * rows * width, transcendentals=0
        ),
        name="assemble",
    )(order, *pieces)


def shards(
    student_bytes, student_weight, teacher_rows, teacher_weight, span_lengths, span_scale, positives
):
    span_dev = span_scale.shape[0]
    embed_width = student_weight.shape[1]
    lanes = lax.axis_size("narrow")
    blocks = lax.axis_size("blk")
    chips = blocks // 2
    lane = lax.axis_index("narrow")
    block = lax.axis_index("blk")
    core = lax.rem(block, 2)
    chip = lax.div(block, 2)
    span_block = span_dev * lanes
    byte_dev = student_bytes.shape[0]
    feats = teacher_rows.shape[1]
    half = feats // 2

    own_half = lax.dynamic_slice_in_dim(teacher_rows, core * half, half, 1)
    sibling_half = sibling(lax.dynamic_slice_in_dim(teacher_rows, (1 - core) * half, half, 1))

    spread = jnp.arange(MOST_BYTES, dtype=jnp.int32)
    edge_bytes = jnp.concatenate(
        [
            lax.ppermute(student_bytes[-MOST_BYTES:], "narrow", [(i, i + 1) for i in range(lanes - 1)]),
            lax.ppermute(student_bytes[:MOST_BYTES], "narrow", [(i + 1, i) for i in range(lanes - 1)]),
        ],
        axis=0,
    )

    teacher_part = jnp.dot(teacher_rows, teacher_weight, preferred_element_type=F32)
    student_bytes, teacher_part = lax.optimization_barrier((student_bytes, teacher_part))
    teacher_proj = lax.psum_scatter(teacher_part, "narrow", scatter_dimension=0, tiled=True)

    small = gather_narrow(jnp.stack([span_scale / embed_width, positives.astype(F32)]))
    small = small.transpose(1, 0, 2).reshape(2, span_block)
    ahead_small, mixed_small = following(small)
    other_small = following_other(small)

    byte_lengths = span_lengths[0]
    byte_ends = jnp.cumsum(byte_lengths)
    byte_starts = byte_ends - byte_lengths

    def owner_order(values):
        return values.reshape(span_dev, lanes).T.reshape(span_block)

    lengths = owner_order(byte_lengths)
    ends = owner_order(byte_ends)
    starts = owner_order(byte_starts)
    lengths_f = lengths.astype(F32)[:, None]
    first = lane * byte_dev
    last = first + byte_dev
    byte_pos = first + jnp.arange(byte_dev, dtype=jnp.int32)
    span_table = (
        (byte_pos[None, :] >= starts[:, None]) & (byte_pos[None, :] < ends[:, None])
    ).astype(BF16)
    edge_pos = jnp.concatenate([first - MOST_BYTES + spread, last + spread])
    edge_table = (
        (edge_pos[None, :] >= starts[:, None]) & (edge_pos[None, :] < ends[:, None])
    ).astype(BF16)
    projected = jnp.dot(student_bytes, student_weight, preferred_element_type=F32).astype(BF16)
    projected_edge = jnp.dot(edge_bytes, student_weight, preferred_element_type=F32).astype(BF16)
    pooled = jnp.dot(span_table, projected, preferred_element_type=F32) + jnp.dot(
        edge_table, projected_edge, preferred_element_type=F32
    )
    student_full, student_rms = normalize(pooled / lengths_f)
    begins_here = (starts >= first) & (starts < last)
    student_sparse = jnp.where(begins_here[:, None], student_full, 0.0).astype(BF16)
    student_shard = scatter_narrow(student_sparse, span_dev)
    student_shard, teacher_proj = lax.optimization_barrier((student_shard, teacher_proj))
    student = lax.all_gather(student_shard, "narrow", axis=0, tiled=True)

    teacher_full, teacher_rms = normalize(teacher_proj)
    teacher = teacher_full.astype(BF16)
    others = jnp.concatenate(
        [permute_blk(teacher, lambda i, k=k: i + k) for k in range(1, STOPS)], axis=0
    )
    keys = jnp.concatenate([teacher, others], axis=0)
    window_small = [small, ahead_small, mixed_small, other_small]
    teacher, student, keys, others, own_half, *window_small = lax.optimization_barrier(
        (teacher, student, keys, others, own_half, *window_small)
    )
    factor, positive = window_small[0][0], window_small[0][1]
    teacher_block = lax.all_gather(teacher, "narrow", axis=0, tiled=True)

    ahead, mixed = following(student)
    mixed_stop = jnp.where(core == 1, 3, 1)
    window_stops = [jnp.int32(0), jnp.int32(2), mixed_stop, 4 - mixed_stop]

    near = jnp.arange(STOPS * span_dev, dtype=jnp.int32)
    near = (near // span_dev) * span_block + lane * span_dev + near % span_dev
    hit = near.astype(F32)[None, :] == positive[:, None]
    scores = contract_last(student, keys) * factor[:, None]
    picked = jnp.sum(jnp.where(hit, scores, 0.0), axis=1)
    row_max = jnp.max(scores, axis=1)
    row_sum = jnp.sum(jnp.exp(scores - row_max[:, None]), axis=1)
    rms_row = jnp.pad(teacher_rms[:, 0], (0, span_block - span_dev))
    stats = gather_narrow(jnp.stack([row_max, row_sum, picked, rms_row]))
    block_rms = stats[:, 3, :span_dev].reshape(span_block, 1)
    top = jnp.max(stats[:, 0], axis=0)
    log_total = top + jnp.log(jnp.sum(stats[:, 1] * jnp.exp(stats[:, 0] - top), axis=0))
    loss = jnp.sum(log_total - jnp.sum(stats[:, 2], axis=0))
    note = jnp.concatenate([log_total, jnp.broadcast_to(loss, (128,))])
    notes = [note, *following(note), following_other(note)]
    ahead, *notes = lax.optimization_barrier((ahead, *notes))
    student_window = [student, ahead, mixed, sibling(ahead)]
    window_log_total = [x[:span_block] for x in notes]

    others, log_total = lax.optimization_barrier((others, log_total))
    others = lax.all_gather(others, "narrow", axis=0)

    small = jnp.stack(
        [x[0] for x in window_small]
        + window_log_total
        + [x[1] - (stop * span_block).astype(F32) for x, stop in zip(window_small, window_stops)]
    )
    teacher_grads = teacher_grads_of(teacher_block, block_rms, student_window, small)
    sibling_grads = sibling(teacher_grads)

    weight_part = contract_first(own_half, teacher_grads)
    weight_part, sibling_grads = lax.optimization_barrier((weight_part, sibling_grads))
    weight_part = weight_part + contract_first(sibling_half, sibling_grads)
    slice_rows = half // chips
    narrowed = weight_part.astype(BF16)
    total = lax.dynamic_slice_in_dim(weight_part, chip * slice_rows, slice_rows, 0)
    spots = jnp.arange(128, dtype=jnp.int32)
    terms = jnp.zeros((128,), F32)
    for x, stop in zip(notes, window_stops):
        terms = jnp.where(spots == lax.rem(block + stop, blocks), x[span_block:], terms)
    own_terms, total = lax.optimization_barrier((terms, total))
    for by in range(4, blocks, 4):
        terms = terms + permute_blk(own_terms, lambda i, by=by: i - by)
    loss_mean = jnp.sum(terms) / (span_block * blocks)

    came = []
    for by in range(1, chips):
        target = lax.rem(chip + by, chips)
        piece = lax.dynamic_slice_in_dim(narrowed, target * slice_rows, slice_rows, 0)
        came.append(permute_blk(piece, lambda i, by=by: i + 2 * by))
    for piece in came:
        total = total + piece.astype(F32)
    total = (total + 0.0 * loss_mean).astype(BF16)
    place = positive.astype(jnp.int32)
    stop, place = place // span_block, place % span_block
    at_lane, at_row = place // span_dev, place % span_dev
    columns = [jnp.where(stop == 0, place, -1)] + [
        jnp.where((stop > 0) & (at_lane == i), (stop - 1) * span_dev + at_row, -1)
        for i in range(lanes)
    ]
    scalars = jnp.stack(
        [factor, log_total + 0.0 * weight_part[0, 0], student_rms[:, 0], lengths_f[:, 0]]
        + [x.astype(F32) for x in columns],
        axis=1,
    )
    span_grad = span_grads_of(student, student_full, scalars, teacher_block, others)
    byte_grad = contract_first(span_table, span_grad).astype(BF16)
    grad_bytes = contract_last(byte_grad, student_weight).astype(BF16)

    pieces = []
    order = []
    for by in range(chips):
        piece = total if by == 0 else permute_blk(total, lambda i, by=by: i + 2 * by)
        if by > 0:
            made = span_grad if by == chips - 1 else grad_bytes
            piece, _ = lax.optimization_barrier((piece, made))
        pieces += [piece, sibling(piece)]
        at = lax.rem(chip + chips - by, chips)
        order += [core * chips + at, (1 - core) * chips + at]
    grad_weight = assembled(jnp.stack(order), pieces)
    return (loss_mean, grad_bytes, grad_weight)


def solution(mesh):
    return jax.shard_map(
        shards,
        mesh=mesh,
        in_specs=(
            P(("blk", "narrow"), None),
            P(),
            P("blk", "narrow"),
            P("narrow", None),
            P("blk", None),
            P(("blk", "narrow")),
            P(("blk", "narrow")),
        ),
        out_specs=(P(), P(("blk", "narrow"), None), P("narrow", None)),
        check_vma=False,
    )
```

```python
import functools

import jax
import jax.numpy as jnp
from jax import lax
from jax.experimental import pallas as pl
from jax.experimental.pallas import tpu as pltpu
from jax.sharding import PartitionSpec as P

STOPS = 4
VMEM_LIMIT = 40 * 1024 * 1024
MOST_BYTES = 16
EPS = 1e-06
BF16 = jnp.bfloat16
F32 = jnp.float32


def normalize(values):
    inv_rms = lax.rsqrt(jnp.mean(values * values, axis=-1, keepdims=True) + EPS)
    return (values * inv_rms, inv_rms)


def norm_back(upstream, normed, inv_rms):
    inner_mean = jnp.mean(upstream * normed, axis=-1, keepdims=True)
    return inv_rms * (upstream - normed * inner_mean)


def contract_first(left, right):
    return lax.dot_general(left, right, (((0,), (0,)), ((), ())), preferred_element_type=F32)


def contract_last(left, right):
    return lax.dot_general(left, right, (((1,), (1,)), ((), ())), preferred_element_type=F32)


def permute_blk(x, target):
    count = lax.axis_size("blk")
    return lax.ppermute(x, "blk", [(i, target(i) % count) for i in range(count)])


def sibling(x):
    return permute_blk(x, lambda i: i ^ 1)


def gather_narrow(x):
    count = lax.axis_size("narrow")
    index = lax.axis_index("narrow")
    out = jnp.zeros((count,) + x.shape, x.dtype)
    out = lax.dynamic_update_index_in_dim(out, x, index, 0)
    for by in range(1, count):
        came = lax.ppermute(x, "narrow", [(i, (i + by) % count) for i in range(count)])
        out = lax.dynamic_update_index_in_dim(out, came, lax.rem(index + count - by, count), 0)
    return out


def following(x):
    ahead = permute_blk(x, lambda i: i - 2)
    mixed = permute_blk(x, lambda i: i - 1 if i % 2 else i - 3)
    return ahead, mixed


def following_other(x):
    return permute_blk(x, lambda i: i - 3 if i % 2 else i - 1)


def scatter_narrow(x, rows):
    count = lax.axis_size("narrow")
    index = lax.axis_index("narrow")
    total = lax.dynamic_slice_in_dim(x, index * rows, rows, 0)
    for by in range(1, count):
        target = lax.rem(index + by, count)
        piece = lax.dynamic_slice_in_dim(x, target * rows, rows, 0)
        total += lax.ppermute(piece, "narrow", [(i, (i + by) % count) for i in range(count)])
    return total


def teacher_terms(rows, stops, teacher, small_ref, windows):
    dteacher = None
    for at, ref in zip(stops, windows):
        scale = small_ref[at : at + 1, :]
        log_total = small_ref[4 + at : 5 + at, :]
        column = small_ref[8 + at : 9 + at, :].astype(jnp.int32)
        scores = contract_last(teacher, ref[...]) * scale
        here = lax.broadcasted_iota(jnp.int32, scores.shape, 0) + pl.program_id(0) * rows
        hit = jnp.where(here == column, 1.0, 0.0)
        grads = ((jnp.exp(scores - log_total) - hit) * scale).astype(BF16)
        term = jnp.dot(grads, ref[...], preferred_element_type=F32)
        dteacher = term if dteacher is None else dteacher + term
    return dteacher


def teacher_first(rows, stops, teacher_ref, small_ref, *refs):
    refs[-1][...] = teacher_terms(rows, stops, teacher_ref[...], small_ref, refs[:-1])


def teacher_last(rows, stops, teacher_ref, small_ref, sum_ref, rms_ref, *refs):
    teacher = teacher_ref[...]
    dteacher = sum_ref[...] + teacher_terms(rows, stops, teacher, small_ref, refs[:-1])
    full = teacher.astype(F32)
    inner_mean = jnp.mean(dteacher * full, axis=-1, keepdims=True)
    refs[-1][...] = (rms_ref[...] * (dteacher - full * inner_mean)).astype(BF16)


def teacher_grads_of(teacher, rms, window, small):
    span_block, width = teacher.shape
    rows = 256
    whole = pl.BlockSpec((span_block, width), lambda i: (0, 0))
    part = pl.BlockSpec((rows, width), lambda i: (i, 0))
    scalars = pl.BlockSpec(small.shape, lambda i: (0, 0))

    def call(body, stops, extra_specs, extra, out_type, name):
        return pl.pallas_call(
            functools.partial(body, rows, stops),
            grid=(span_block // rows,),
            in_specs=[part, scalars] + extra_specs + [whole] * len(stops),
            out_specs=part,
            out_shape=jax.ShapeDtypeStruct((span_block, width), out_type),
            compiler_params=pltpu.CompilerParams(vmem_limit_bytes=VMEM_LIMIT),
            cost_estimate=pl.CostEstimate(
                flops=4 * len(stops) * span_block * span_block * width,
                bytes_accessed=(8 + 2 * len(stops)) * span_block * width,
                transcendentals=len(stops) * span_block * span_block,
            ),
            name=name,
        )(teacher, small, *extra, *[window[at] for at in stops])

    dteacher = call(teacher_first, (0, 1, 3), [], (), F32, "teacher_first")
    rms_spec = pl.BlockSpec((rows, 1), lambda i: (i, 0))
    return call(teacher_last, (2,), [part, rms_spec], (dteacher, rms), BF16, "teacher_last")


def student_side(student_ref, full_ref, scalar_ref, own_ref, others_ref, out_ref):
    student = student_ref[...]
    scale = scalar_ref[:, 0:1]
    log_total = scalar_ref[:, 1:2]

    def term(keys, at):
        column = scalar_ref[:, 4 + at : 5 + at].astype(jnp.int32)
        scores = contract_last(student, keys) * scale
        here = lax.broadcasted_iota(jnp.int32, scores.shape, 1)
        hit = jnp.where(here == column, 1.0, 0.0)
        grads = ((jnp.exp(scores - log_total) - hit) * scale).astype(BF16)
        return jnp.dot(grads, keys, preferred_element_type=F32)

    dstudent = term(own_ref[...], 0)
    for at in range(others_ref.shape[0]):
        dstudent = dstudent + term(others_ref[at], 1 + at)
    full = full_ref[...]
    inner_mean = jnp.mean(dstudent * full, axis=-1, keepdims=True)
    grad = scalar_ref[:, 2:3] * (dstudent - full * inner_mean) / scalar_ref[:, 3:4]
    out_ref[...] = grad.astype(BF16)


def span_grads_of(student, full, scalars, own, others):
    span_block, width = student.shape
    rows = 256
    part = pl.BlockSpec((rows, width), lambda i: (i, 0))
    return pl.pallas_call(
        student_side,
        grid=(span_block // rows,),
        in_specs=[
            part,
            part,
            pl.BlockSpec((rows, scalars.shape[1]), lambda i: (i, 0)),
            pl.BlockSpec(own.shape, lambda i: (0, 0)),
            pl.BlockSpec(others.shape, lambda i: (0, 0, 0)),
        ],
        out_specs=part,
        out_shape=jax.ShapeDtypeStruct((span_block, width), BF16),
        compiler_params=pltpu.CompilerParams(vmem_limit_bytes=48 * 1024 * 1024),
        cost_estimate=pl.CostEstimate(
            flops=16 * span_block * span_block * width,
            bytes_accessed=16 * span_block * width,
            transcendentals=4 * span_block * span_block,
        ),
        name="student_side",
    )(student, full, scalars, own, others)


def assemble(order_ref, *refs):
    for at, ref in enumerate(refs[:-1]):

        @pl.when(pl.program_id(0) == at)
        def _(ref=ref):
            refs[-1][...] = ref[...].astype(F32)


def assembled(order, pieces):
    rows, width = pieces[0].shape
    count = len(pieces)
    return pl.pallas_call(
        assemble,
        grid_spec=pltpu.PrefetchScalarGridSpec(
            num_scalar_prefetch=1,
            grid=(count,),
            in_specs=[pl.BlockSpec((rows, width), lambda i, order: (0, 0))] * count,
            out_specs=pl.BlockSpec((rows, width), lambda i, order: (order[i], 0)),
        ),
        out_shape=jax.ShapeDtypeStruct((count * rows, width), F32),
        compiler_params=pltpu.CompilerParams(vmem_limit_bytes=32 * 1024 * 1024),
        cost_estimate=pl.CostEstimate(
            flops=count * rows * width, bytes_accessed=6 * count * rows * width, transcendentals=0
        ),
        name="assemble",
    )(order, *pieces)


def shards(
    student_bytes, student_weight, teacher_rows, teacher_weight, span_lengths, span_scale, positives
):
    span_dev = span_scale.shape[0]
    embed_width = student_weight.shape[1]
    lanes = lax.axis_size("narrow")
    blocks = lax.axis_size("blk")
    chips = blocks // 2
    lane = lax.axis_index("narrow")
    block = lax.axis_index("blk")
    core = lax.rem(block, 2)
    chip = lax.div(block, 2)
    span_block = span_dev * lanes
    byte_dev = student_bytes.shape[0]
    feats = teacher_rows.shape[1]
    half = feats // 2

    own_half = lax.dynamic_slice_in_dim(teacher_rows, core * half, half, 1)
    sibling_half = sibling(lax.dynamic_slice_in_dim(teacher_rows, (1 - core) * half, half, 1))

    spread = jnp.arange(MOST_BYTES, dtype=jnp.int32)
    edge_bytes = jnp.concatenate(
        [
            lax.ppermute(student_bytes[-MOST_BYTES:], "narrow", [(i, i + 1) for i in range(lanes - 1)]),
            lax.ppermute(student_bytes[:MOST_BYTES], "narrow", [(i + 1, i) for i in range(lanes - 1)]),
        ],
        axis=0,
    )

    teacher_part = jnp.dot(teacher_rows, teacher_weight, preferred_element_type=F32)
    student_bytes, teacher_part = lax.optimization_barrier((student_bytes, teacher_part))
    teacher_proj = lax.psum_scatter(teacher_part, "narrow", scatter_dimension=0, tiled=True)

    small = gather_narrow(jnp.stack([span_scale / embed_width, positives.astype(F32)]))
    small = small.transpose(1, 0, 2).reshape(2, span_block)
    ahead_small, mixed_small = following(small)
    other_small = following_other(small)

    byte_lengths = span_lengths[0]
    byte_ends = jnp.cumsum(byte_lengths)
    byte_starts = byte_ends - byte_lengths

    def owner_order(values):
        return values.reshape(span_dev, lanes).T.reshape(span_block)

    lengths = owner_order(byte_lengths)
    ends = owner_order(byte_ends)
    starts = owner_order(byte_starts)
    lengths_f = lengths.astype(F32)[:, None]
    first = lane * byte_dev
    last = first + byte_dev
    byte_pos = first + jnp.arange(byte_dev, dtype=jnp.int32)
    span_table = (
        (byte_pos[None, :] >= starts[:, None]) & (byte_pos[None, :] < ends[:, None])
    ).astype(BF16)
    edge_pos = jnp.concatenate([first - MOST_BYTES + spread, last + spread])
    edge_table = (
        (edge_pos[None, :] >= starts[:, None]) & (edge_pos[None, :] < ends[:, None])
    ).astype(BF16)
    projected = jnp.dot(student_bytes, student_weight, preferred_element_type=F32).astype(BF16)
    projected_edge = jnp.dot(edge_bytes, student_weight, preferred_element_type=F32).astype(BF16)
    pooled = jnp.dot(span_table, projected, preferred_element_type=F32) + jnp.dot(
        edge_table, projected_edge, preferred_element_type=F32
    )
    student_full, student_rms = normalize(pooled / lengths_f)
    begins_here = (starts >= first) & (starts < last)
    student_sparse = jnp.where(begins_here[:, None], student_full, 0.0).astype(BF16)
    student_shard = scatter_narrow(student_sparse, span_dev)
    student_shard, teacher_proj = lax.optimization_barrier((student_shard, teacher_proj))
    student = lax.all_gather(student_shard, "narrow", axis=0, tiled=True)

    teacher_full, teacher_rms = normalize(teacher_proj)
    teacher = teacher_full.astype(BF16)
    others = jnp.concatenate(
        [permute_blk(teacher, lambda i, k=k: i + k) for k in range(1, STOPS)], axis=0
    )
    keys = jnp.concatenate([teacher, others], axis=0)
    window_small = [small, ahead_small, mixed_small, other_small]
    teacher, student, keys, others, own_half, *window_small = lax.optimization_barrier(
        (teacher, student, keys, others, own_half, *window_small)
    )
    factor, positive = window_small[0][0], window_small[0][1]
    teacher_block = lax.all_gather(teacher, "narrow", axis=0, tiled=True)

    ahead, mixed = following(student)
    mixed_stop = jnp.where(core == 1, 3, 1)
    window_stops = [jnp.int32(0), jnp.int32(2), mixed_stop, 4 - mixed_stop]

    near = jnp.arange(STOPS * span_dev, dtype=jnp.int32)
    near = (near // span_dev) * span_block + lane * span_dev + near % span_dev
    hit = near.astype(F32)[None, :] == positive[:, None]
    scores = contract_last(student, keys) * factor[:, None]
    picked = jnp.sum(jnp.where(hit, scores, 0.0), axis=1)
    row_max = jnp.max(scores, axis=1)
    row_sum = jnp.sum(jnp.exp(scores - row_max[:, None]), axis=1)
    rms_row = jnp.pad(teacher_rms[:, 0], (0, span_block - span_dev))
    stats = gather_narrow(jnp.stack([row_max, row_sum, picked, rms_row]))
    block_rms = stats[:, 3, :span_dev].reshape(span_block, 1)
    top = jnp.max(stats[:, 0], axis=0)
    log_total = top + jnp.log(jnp.sum(stats[:, 1] * jnp.exp(stats[:, 0] - top), axis=0))
    loss = jnp.sum(log_total - jnp.sum(stats[:, 2], axis=0))
    note = jnp.concatenate([log_total, jnp.broadcast_to(loss, (128,))])
    notes = [note, *following(note), following_other(note)]
    ahead, *notes = lax.optimization_barrier((ahead, *notes))
    student_window = [student, ahead, mixed, sibling(ahead)]
    window_log_total = [x[:span_block] for x in notes]

    others, log_total = lax.optimization_barrier((others, log_total))
    others = lax.all_gather(others, "narrow", axis=0)

    small = jnp.stack(
        [x[0] for x in window_small]
        + window_log_total
        + [x[1] - (stop * span_block).astype(F32) for x, stop in zip(window_small, window_stops)]
    )
    teacher_grads = teacher_grads_of(teacher_block, block_rms, student_window, small)
    sibling_grads = sibling(teacher_grads)

    weight_part = contract_first(own_half, teacher_grads)
    weight_part, sibling_grads = lax.optimization_barrier((weight_part, sibling_grads))
    weight_part = weight_part + contract_first(sibling_half, sibling_grads)
    slice_rows = half // chips
    narrowed = weight_part.astype(BF16)
    total = lax.dynamic_slice_in_dim(weight_part, chip * slice_rows, slice_rows, 0)
    spots = jnp.arange(128, dtype=jnp.int32)
    terms = jnp.zeros((128,), F32)
    for x, stop in zip(notes, window_stops):
        terms = jnp.where(spots == lax.rem(block + stop, blocks), x[span_block:], terms)
    own_terms, total = lax.optimization_barrier((terms, total))
    for by in range(4, blocks, 4):
        terms = terms + permute_blk(own_terms, lambda i, by=by: i - by)

    came = []
    for by in range(1, chips):
        target = lax.rem(chip + by, chips)
        piece = lax.dynamic_slice_in_dim(narrowed, target * slice_rows, slice_rows, 0)
        came.append(permute_blk(piece, lambda i, by=by: i + 2 * by))
    *came, terms = lax.optimization_barrier((*came, terms))
    loss_mean = jnp.sum(terms) / (span_block * blocks)
    for piece in came:
        total = total + piece.astype(F32)
    total = total.astype(BF16)
    place = positive.astype(jnp.int32)
    stop, place = place // span_block, place % span_block
    at_lane, at_row = place // span_dev, place % span_dev
    columns = [jnp.where(stop == 0, place, -1)] + [
        jnp.where((stop > 0) & (at_lane == i), (stop - 1) * span_dev + at_row, -1)
        for i in range(lanes)
    ]
    scalars = jnp.stack(
        [factor, log_total + 0.0 * weight_part[0, 0], student_rms[:, 0], lengths_f[:, 0]]
        + [x.astype(F32) for x in columns],
        axis=1,
    )
    span_grad = span_grads_of(student, student_full, scalars, teacher_block, others)
    byte_grad = contract_first(span_table, span_grad).astype(BF16)
    grad_bytes = contract_last(byte_grad, student_weight).astype(BF16)

    pieces = []
    order = []
    for by in range(chips):
        piece = total if by == 0 else permute_blk(total, lambda i, by=by: i + 2 * by)
        if by > 0:
            made = span_grad if by == chips - 1 else grad_bytes
            piece, _ = lax.optimization_barrier((piece, made))
        pieces += [piece, sibling(piece)]
        at = lax.rem(chip + chips - by, chips)
        order += [core * chips + at, (1 - core) * chips + at]
    grad_weight = assembled(jnp.stack(order), pieces)
    return (loss_mean, grad_bytes, grad_weight)


def solution(mesh):
    return jax.shard_map(
        shards,
        mesh=mesh,
        in_specs=(
            P(("blk", "narrow"), None),
            P(),
            P("blk", "narrow"),
            P("narrow", None),
            P("blk", None),
            P(("blk", "narrow")),
            P(("blk", "narrow")),
        ),
        out_specs=(P(), P(("blk", "narrow"), None), P("narrow", None)),
        check_vma=False,
    )
```
